1024 devices in a mesh: section: 8 (over z_hi, core), expert: 32 (over y, z_lo), dp: 4 (over x).
Axes of the slice: x: 4, y: 8, z: 16 (z_hi: 4, z_lo: 4; z = z_hi * 4 + z_lo), core: 2. Of those that a mesh axis runs over, the one named last changes fastest.
Arguments:
- tokens: bfloat16 [16384, 2048], P(('dp', 'expert')), parts along dimension 0, may hold values from -6 to 6
- routes: int32 [16384, 2], P(('dp', 'expert')), parts along dimension 0, may hold values from 0 to 63, all different within a row; in each aligned block of 128 rows (0 to 127, 128 to 255, ...) at most 8 rows name the same one
- gates: bfloat16 [16384, 2], P(('dp', 'expert')), parts along dimension 0, may hold values from 0.19921875 to 1
- fc_in: bfloat16 [64, 2048, 4096], P('expert', None, 'section'), may hold values from -0.125 to 0.125
- fc_out: bfloat16 [64, 4096, 2048], P('expert', 'section'), may hold values from -0.09375 to 0.09375
- norm_gain: float32 [2048], replicated, may hold values from 0.5 to 1.5
- norm_bias: float32 [2048], replicated, may hold values from -3 to 3
- key_weight: bfloat16 [2048, 1024], P(None, 'section'), may hold values from -0.125 to 0.125
- value_weight: bfloat16 [2048, 1024], P(None, 'section'), may hold values from -0.125 to 0.125
- queries: bfloat16 [16384, 1024], P(('dp', 'expert'), 'section'), parts along dimension 0, may hold values from -160 to 160
- source_len: int32 [128], P(('dp', 'expert')), parts along dimension 0, may hold values from 32 to 128
- target_len: int32 [128], P(('dp', 'expert')), parts along dimension 0, may hold values from 32 to 128
Outputs:
- context: bfloat16 [16384, 1024], P(('dp', 'expert'), 'section'), parts along dimension 0
The draws below stay inside these ranges and needn't reach their ends.
There are 4 independent parts, one for each index of `dp`. The reference program is written for one: setup_inputs(seed, part) draws one part's arguments, and reference() takes and returns one part's arrays. A program takes and returns all parts, laid end to end along the dimension named above; an argument that names none is the same for every part. Nothing has to cross between parts.
Inputs may be any that keep to these rules, and one draw needn't show every extreme that they name: `routes`: each row names two different experts. The 128 rows of one index of expert name one expert at most 8 times, a bound that some block reaches.
All inputs are finite; a program needn't handle non-finite values.
Results may differ from the reference program's by a relative error of at most 0.04.
Values may be sent and summed in bfloat16 or wider, within the bound.
A program may use at most 64 MiB of HBM per device.

```python
import math
import jax
import jax.numpy as jnp
import numpy as np
from jax import lax

D = 2048
FF = 4096
HEADS = 8
HEAD_DIM = 128
SRC = 128
TGT = 128
EXPERTS = 64
TOK_DEV = 128
CAP = 8
TOKENS = 4096
SENTENCES = 32
TGT_TOKENS = 4096
N_SECTION = 8


def draw_queries(key, part):
    key = jax.random.fold_in(key, 11)
    shape = (TGT_TOKENS, HEADS * HEAD_DIM)
    return jnp.clip(jax.random.normal(key, shape, jnp.float32), -4.0, 4.0).astype(jnp.bfloat16)


def place_ends(array, rng, smallest, high):
    longest = array.shape.index(max(array.shape))
    spots = []
    for shift in (0, 1):
        where = [jax.random.randint(jax.random.fold_in(rng, axis), (), 0, length) for axis, length in enumerate(array.shape)]
        where[longest] = (where[longest] + shift) % array.shape[longest]
        spots.append(tuple(where))
    return array.at[spots[0]].set(smallest).at[spots[1]].set(high)


def shard_levels(key, extent, cuts, smallest, top_value):
    loudness, own = 1.0, jax.random.fold_in(key, 6)
    for position, blocks in cuts:
        draws = jnp.exp(jax.random.uniform(jax.random.fold_in(own, position), (blocks,), jnp.float32, smallest / len(cuts), top_value / len(cuts)))
        loudness = loudness * jnp.repeat(draws, extent[position] // blocks).reshape([-1 if axis == position else 1 for axis in range(len(extent))])
    return loudness


def assign_block(key, own, number, rows, count, top, limit, slope):
    ranking = jax.random.permutation(key, count)
    packed, usual = portions_of(count, rows * top, limit, slope, True), portions_of(count, rows * top, limit, slope, False)
    places = jnp.arange(count)

    def named(tallies, turn):
        used = int((tallies > 0).sum())
        fixed = max(1, used // 4)
        shifted = fixed + (places - fixed + turn * (used - fixed)) % max(1, count - fixed)
        return jnp.zeros((count,), jnp.int32).at[ranking[jnp.where(places < fixed, places, shifted)]].set(jnp.asarray(tallies, jnp.int32))

    tallies = jnp.where(number % 4 == 0, named(packed, number // 4), named(usual, number - number // 4 - 1))
    mixed = jax.random.permutation(jax.random.fold_in(own, 3), count)
    donor, receiver = mixed[0:count // 2 * 2:2], mixed[1:count // 2 * 2:2]
    room = jnp.minimum(tallies[donor] - 1, limit - tallies[receiver]) // 2
    room = jnp.where((donor == ranking[0]) | (receiver == ranking[0]) | (tallies[receiver] == 0), 0, jnp.maximum(room, 0))
    shifted = jax.random.randint(jax.random.fold_in(own, 4), (count // 2,), 0, 1 << 20) % (room + 1)
    tallies = tallies.at[donor].add(-shifted).at[receiver].add(shifted)
    members = jnp.searchsorted(jnp.cumsum(tallies), jnp.arange(rows * top), side="right").astype(jnp.int32)
    table = members.reshape(top, rows).T
    table = table[jax.random.permutation(jax.random.fold_in(own, 1), rows)]
    turn = jax.random.randint(jax.random.fold_in(own, 2), (rows, 1), 0, top)
    return jnp.take_along_axis(table, (jnp.arange(top)[None, :] + turn) % top, axis=1)


def portions_of(count, total, reach, lean, full):
    portions = [(1 << 20) // math.isqrt(standing ** lean) + 1 for standing in range(1, count + 1)]
    largest = reach if full else min(reach, max(-(-total // count), total * portions[0] // sum(portions)))
    least = 1 if total - largest >= count - 1 else 0
    holding, rest = [largest] + [least] * (count - 1), total - largest - least * (count - 1)
    while rest > 0:
        candidates = [i for i in range(1, count) if holding[i] < largest] or [i for i in range(1, count) if holding[i] < reach]
        pool, remaining = sum([portions[i] for i in candidates]), rest
        for i in candidates:
            more = min(reach - holding[i], max(1, remaining * portions[i] // pool), rest)
            holding[i] = holding[i] + more
            rest = rest - more
    return np.array(holding)


def bell_draw(own_key, dims, deviation, reach, cuts=(), kind=jnp.bfloat16):
    level = shard_levels(own_key, dims, cuts, -0.22, 0.18) if cuts else 1.0
    entries = jax.random.normal(own_key, dims, jnp.float32) * deviation * level
    return jnp.minimum(jnp.maximum(entries, -reach), reach).astype(kind)


def setup_inputs(seed: int = 0, part: int = 0) -> dict:
    streams_of = jax.random.split(jax.random.key(seed), 13)
    part_splits = jax.random.split(jax.random.fold_in(streams_of[12], part), 13)
    tokens = bell_draw(part_splits[0], (TOKENS, D), 1.0, 6.0, ((0, 32),))
    routes_keys = jax.random.split(jax.random.fold_in(part_splits[1], 1), TOKENS // TOK_DEV)
    routes_turns = jax.random.permutation(jax.random.fold_in(part_splits[1], 3), TOKENS // TOK_DEV)
    routes = jax.vmap(lambda own, number: assign_block(jax.random.fold_in(part_splits[1], 2), own, number, TOK_DEV, EXPERTS, 2, CAP, 2))(routes_keys, routes_turns).reshape((TOKENS, 2))
    gates = jnp.clip(0.19921875 + 0.80078125 * jax.random.uniform(part_splits[2], (TOKENS, 2), jnp.float32) ** shard_levels(part_splits[2], (TOKENS, 2), ((0, 32),), -0.2, 0.2), 0.19921875, 1.0).astype(jnp.bfloat16)
    fc_in = bell_draw(streams_of[3], (EXPERTS, D, FF), D ** -0.5, 0.125, ((0, 32), (2, 8)))
    fc_out = bell_draw(streams_of[4], (EXPERTS, FF, D), FF ** -0.5, 0.09375, ((0, 32), (1, 8)))
    norm_gain = jnp.clip(1.0 + 0.1 * jax.random.normal(streams_of[5], (D,), jnp.float32), 0.5, 1.5)
    norm_bias = bell_draw(streams_of[6], (D,), 0.5, 3.0, (), jnp.float32)
    key_weight = bell_draw(streams_of[7], (D, HEADS * HEAD_DIM), D ** -0.5, 0.125, ((1, 8),))
    value_weight = bell_draw(streams_of[8], (D, HEADS * HEAD_DIM), D ** -0.5, 0.125, ((1, 8),))
    queries = draw_queries(jax.random.fold_in(jax.random.fold_in(streams_of[12], part), 71), part)
    source_len = place_ends(jax.random.randint(part_splits[10], (SENTENCES,), SRC // 4, SRC + 1), jax.random.fold_in(part_splits[10], 1), SRC // 4, SRC).astype(jnp.int32)
    target_len = place_ends(jax.random.randint(part_splits[11], (SENTENCES,), TGT // 4, TGT + 1), jax.random.fold_in(part_splits[11], 1), TGT // 4, TGT).astype(jnp.int32)
    return dict(tokens=tokens, routes=routes, gates=gates, fc_in=fc_in, fc_out=fc_out, norm_gain=norm_gain, norm_bias=norm_bias, key_weight=key_weight, value_weight=value_weight, queries=queries, source_len=source_len, target_len=target_len)


def normalize(summed, norm_gain, norm_bias):
    center = summed - lax.optimization_barrier(jnp.mean(summed, axis=-1, keepdims=True))
    spread = lax.optimization_barrier(jnp.mean(center * center, axis=-1, keepdims=True))
    return (center * lax.rsqrt(spread + 1e-05) * norm_gain + norm_bias).astype(jnp.bfloat16)

def reference(tokens, routes, gates, fc_in, fc_out, norm_gain, norm_bias, key_weight, value_weight, queries, source_len, target_len):
    blocks = TOKENS // TOK_DEV
    pair_ids = routes.reshape(blocks, TOK_DEV * 2)
    onehot = (pair_ids[:, :, None] == jnp.arange(EXPERTS, dtype=jnp.int32)[None, None, :]).astype(jnp.int32)
    order_rank = lax.optimization_barrier(jnp.sum((jnp.cumsum(onehot, axis=1) - onehot) * onehot, axis=2))
    block_ids = jnp.arange(blocks, dtype=jnp.int32)[:, None]
    slot_index = ((pair_ids * blocks + block_ids) * CAP + order_rank).reshape(-1).astype(jnp.int32)
    token_ids = jnp.repeat(jnp.arange(TOKENS, dtype=jnp.int32), 2)
    buffer = jnp.zeros((EXPERTS * blocks * CAP, D), jnp.bfloat16).at[slot_index].set(tokens[token_ids])
    buffer = buffer.reshape(EXPERTS, blocks * CAP, D)

    def run_expert(operands):
        arrived, weight_in, weight_out = operands
        hidden = jax.nn.relu(jnp.dot(arrived, weight_in, preferred_element_type=jnp.float32)).astype(jnp.bfloat16)
        pieces = jnp.einsum('rbf,bfd->rbd', hidden.reshape(arrived.shape[0], N_SECTION, -1).astype(jnp.float32), weight_out.reshape(N_SECTION, -1, D).astype(jnp.float32))
        rounded = lax.optimization_barrier(pieces.astype(jnp.bfloat16))
        return lax.optimization_barrier(jnp.sum(rounded.astype(jnp.float32), axis=1))
    outputs = lax.map(run_expert, (buffer, fc_in, fc_out)).reshape(-1, D)
    picked = outputs[slot_index].reshape(TOKENS, 2, D)
    mixed = lax.optimization_barrier(jnp.sum(gates.astype(jnp.float32)[:, :, None] * picked, axis=1))
    memory = normalize(tokens.astype(jnp.float32) + mixed, norm_gain, norm_bias)
    key_rows = jnp.dot(memory, key_weight, preferred_element_type=jnp.float32).astype(jnp.bfloat16)
    value_rows = jnp.dot(memory, value_weight, preferred_element_type=jnp.float32).astype(jnp.bfloat16)
    query_grid = queries.reshape(SENTENCES, TGT, HEADS, HEAD_DIM).astype(jnp.float32)
    key_grid = key_rows.reshape(SENTENCES, SRC, HEADS, HEAD_DIM).astype(jnp.float32)
    value_grid = value_rows.reshape(SENTENCES, SRC, HEADS, HEAD_DIM).astype(jnp.float32)
    scores = jnp.einsum('sqhd,skhd->shqk', query_grid, key_grid) * HEAD_DIM ** (-0.5)
    key_mask = jnp.arange(SRC, dtype=jnp.int32)[None, :] < source_len[:, None]
    scores = jnp.where(key_mask[:, None, None, :], scores, -jnp.inf)
    highest = lax.optimization_barrier(jnp.max(scores, axis=-1, keepdims=True))
    expo = jnp.exp(scores - highest)
    weights = (expo / lax.optimization_barrier(jnp.sum(expo, axis=-1, keepdims=True))).astype(jnp.bfloat16)
    context = jnp.einsum('shqk,skhd->sqhd', weights.astype(jnp.float32), value_grid)
    row_mask = jnp.arange(TGT, dtype=jnp.int32)[None, :] < target_len[:, None]
    context = jnp.where(row_mask[:, :, None, None], context, 0.0)
    return context.reshape(TGT_TOKENS, HEADS * HEAD_DIM).astype(jnp.bfloat16)
```

```python
import functools

import jax
import jax.numpy as jnp
from jax import lax
from jax.experimental import pallas as pl
from jax.experimental.pallas import tpu as pltpu
from jax.sharding import PartitionSpec as P

MESH = pl.DeviceIdType.MESH
BF16, F32 = jnp.bfloat16, jnp.float32

HEAD_DIM = 128
ROWS = 128
D = 2048
HALF = 1024
HID = 512
CAP = 8
NY, NZ, NLO = 8, 16, 4
NCH, CW = 2, 512
FIRST = 5
SETS = ((0, FIRST), (FIRST, NY))


def dy_of(m):
    return ((m + 1) // 2) * (1 - 2 * ((m + 1) % 2))


def mirror(m):
    return jnp.where((m == 0) | (m == 7), m, m + 1 - 2 * ((m + 1) % 2))


def dz_of(d, core):
    return d - 4 * ((d + core) // 3)


def kernel(
    tokens, routes, gates, fc_in, fc_out, gain, bias, key_w, value_w, queries, source_len, target_len,
    context,
    outgoing, arrived, rows_in, w_in, w_out, kw, vw, hidden, part, returned, combining,
    mixed_f, mixed_b, scattered, gathered,
    load_sem, disp_s, disp_r, fwd_s, fwd_r, swap_s, swap_r, hid_s, hid_r,
    ret_s, ret_r, rs_s, rs_r, ag_s, ag_r, sib_s, sib_r,
):
    section, group = lax.axis_index("section"), lax.axis_index("expert")
    zhi, core = section // 2, section % 2
    y, zlo = group // NLO, group % NLO
    z = zhi * NLO + zlo
    other = 1 - core

    def device(y2, z2, core2):
        return {"section": (z2 // NLO) * 2 + core2, "expert": y2 * NLO + z2 % NLO}

    def to(m, d):
        return device((y + dy_of(m) + NY) % NY, (z + dz_of(d, core) + NZ) % NZ, core)

    def to_hi(r):
        return device(y, (z + NLO * r) % NZ, core)

    sibling = device(y, z, other)

    loads = [
        pltpu.make_async_copy(fc_in, w_in, load_sem.at[0]),
        pltpu.make_async_copy(
            fc_out.at[:, :, pl.ds(pl.multiple_of(core * HALF, HALF), HALF)], w_out.at[core], load_sem.at[1]
        ),
        pltpu.make_async_copy(key_w, kw, load_sem.at[2]),
        pltpu.make_async_copy(value_w, vw, load_sem.at[3]),
    ]
    for load in loads:
        load.start()

    barrier = pltpu.get_barrier_semaphore()

    def greet(k, carry):
        m, d = k // NLO, k % NLO
        source = device((y - dy_of(m) + NY) % NY, (z - dz_of(d, core) + NZ) % NZ, core)
        pl.semaphore_signal(barrier, inc=1, device_id=source, device_id_type=MESH)
        return carry

    lax.fori_loop(1, NY * NLO, greet, 0)
    for r in range(1, 4):
        pl.semaphore_signal(barrier, inc=1, device_id=to_hi(r), device_id_type=MESH)
    pl.semaphore_signal(barrier, inc=1, device_id=sibling, device_id_type=MESH)

    experts = 2 * NY * NLO
    lane = lax.broadcasted_iota(jnp.int32, (ROWS, experts), 1)
    route0, route1 = routes[:, 0:1], routes[:, 1:2]
    hot0 = jnp.where(lane == route0, 1.0, 0.0)
    hot1 = jnp.where(lane == route1, 1.0, 0.0)
    earlier = jnp.where(
        lax.broadcasted_iota(jnp.int32, (ROWS, ROWS), 0) > lax.broadcasted_iota(jnp.int32, (ROWS, ROWS), 1),
        1.0, 0.0,
    )
    before = jnp.dot(earlier.astype(BF16), (hot0 + hot1).astype(BF16), preferred_element_type=F32)
    slot0 = route0.astype(F32) * CAP + jnp.sum(before * hot0, axis=1, keepdims=True)
    slot1 = route1.astype(F32) * CAP + jnp.sum(before * hot1, axis=1, keepdims=True)
    slots = experts * CAP
    column = lax.broadcasted_iota(jnp.int32, (1, slots), 1)
    m_col = column // (NLO * 2 * CAP)
    d_col = (column // (2 * CAP)) % NLO
    y_col = (y + dy_of(m_col) + NY) % NY
    group_col = y_col * NLO + (zlo + d_col) % NLO
    slot_col = (group_col * (2 * CAP) + column % (2 * CAP)).astype(F32)
    pick0, pick1 = slot0 == slot_col, slot1 == slot_col
    placing = jnp.where(pick0 | pick1, 1.0, 0.0)
    gate0, gate1 = gates[:, 0:1].astype(F32), gates[:, 1:2].astype(F32)
    combining[...] = (jnp.where(pick0, gate0, 0.0) + jnp.where(pick1, gate1, 0.0)).astype(BF16)
    half = tokens[:, pl.ds(pl.multiple_of(core * HALF, HALF), HALF)]
    placed = jnp.dot(placing.T.astype(BF16), half, preferred_element_type=F32).astype(BF16)
    outgoing[...] = placed.reshape(NY, NLO, 2 * CAP, HALF)

    pl.semaphore_wait(barrier, NY * NLO - 1 + 3 + 1)

    def dispatch_copy(m, d):
        return pltpu.make_async_remote_copy(
            src_ref=outgoing.at[m, d],
            dst_ref=arrived.at[core, mirror(m), (NLO - d) % NLO],
            send_sem=disp_s.at[m],
            recv_sem=disp_r.at[mirror(m)],
            device_id=to(m, d),
            device_id_type=MESH,
        )

    def send_dispatch(k, carry):
        dispatch_copy(k // NLO, k % NLO).start()
        return carry

    lax.fori_loop(1, NY * NLO, send_dispatch, 0)
    w_swap = pltpu.make_async_remote_copy(
        src_ref=fc_out.at[:, :, pl.ds(pl.multiple_of(other * HALF, HALF), HALF)],
        dst_ref=w_out.at[core],
        send_sem=swap_s,
        recv_sem=swap_r,
        device_id=sibling,
        device_id_type=MESH,
    )
    arrived[core, 0, 0] = outgoing[0, 0]

    def wait_bytes(ref, sem):
        pltpu.make_async_copy(ref, ref, sem).wait()

    def forward_copy(m):
        return pltpu.make_async_remote_copy(
            src_ref=arrived.at[core, m],
            dst_ref=arrived.at[core, m],
            send_sem=fwd_s.at[m],
            recv_sem=fwd_r.at[m],
            device_id=sibling,
            device_id_type=MESH,
        )

    def hidden_copy(number):
        m0, m1 = SETS[number]
        rows = pl.ds(m0 * NLO * CAP, (m1 - m0) * NLO * CAP)
        return pltpu.make_async_remote_copy(
            src_ref=hidden.at[core, :, rows],
            dst_ref=hidden.at[core, :, rows],
            send_sem=hid_s.at[number],
            recv_sem=hid_r.at[number],
            device_id=sibling,
            device_id_type=MESH,
        )

    def return_copy(ch, m, d):
        return pltpu.make_async_remote_copy(
            src_ref=part.at[ch, m, d],
            dst_ref=returned.at[ch, mirror(m), (NLO - d) % NLO],
            send_sem=ret_s.at[ch, m],
            recv_sem=ret_r.at[ch, mirror(m)],
            device_id=to(m, d),
            device_id_type=MESH,
        )

    w_swap_started = False
    for number, (m0, m1) in enumerate(SETS):
        def take(m, carry):
            wait_bytes(arrived.at[core, m], disp_r.at[m])
            forward_copy(m).start()
            return carry

        if m0 == 0:
            wait_bytes(arrived.at[core, 0, pl.ds(1, NLO - 1)], disp_r.at[0])
            forward_copy(0).start()
        lax.fori_loop(max(m0, 1), m1, take, 0)
        if number == 0:
            w_swap.start()

        def relayout(m, carry):
            wait_bytes(arrived.at[other, m], fwd_r.at[m])
            for h in range(2):
                block = arrived[h, m].astype(F32)
                for i in range(2):
                    rows_in[i, pl.ds(pl.multiple_of(m * NLO * CAP, NLO * CAP), NLO * CAP), h * HALF:(h + 1) * HALF] = (
                        block[:, i * CAP:(i + 1) * CAP, :].reshape(NLO * CAP, HALF).astype(BF16)
                    )
            return carry

        lax.fori_loop(m0, m1, relayout, 0)
        first, count = m0 * NLO * CAP, (m1 - m0) * NLO * CAP
        if number == 0:
            loads[0].wait()
        for i in range(2):
            for n in range(0, HID, 256):
                h = jnp.dot(rows_in[i, first:first + count, :], w_in[i, :, n:n + 256], preferred_element_type=F32)
                hidden[core, i, first:first + count, n:n + 256] = jnp.maximum(h, 0.0).astype(BF16)
        hidden_copy(number).start()
        if number == 0:
            loads[1].wait()
            w_swap.wait()
        hidden_copy(number).wait()
        for ch in range(NCH):
            cols = slice(ch * CW, (ch + 1) * CW)
            sums = [
                jnp.dot(hidden[0, i, first:first + count, :], w_out[0, i, :, cols], preferred_element_type=F32)
                + jnp.dot(hidden[1, i, first:first + count, :], w_out[1, i, :, cols], preferred_element_type=F32)
                for i in range(2)
            ]
            sums = [s.reshape((m1 - m0) * NLO, CAP, CW) for s in sums]
            both = jnp.concatenate(sums, axis=1).astype(BF16)
            part[ch, m0:m1] = both.reshape(m1 - m0, NLO, 2 * CAP, CW)

            def send_return(k, carry):
                return_copy(ch, k // NLO, k % NLO).start()
                return carry

            lax.fori_loop(max(m0 * NLO, 1), m1 * NLO, send_return, 0)
            if m0 == 0:
                returned[ch, 0, 0] = part[ch, 0, 0]

    def scatter_copy(ch, r):
        return pltpu.make_async_remote_copy(
            src_ref=mixed_b.at[ch, (zhi + r) % 4],
            dst_ref=scattered.at[ch, r - 1],
            send_sem=rs_s.at[ch, r - 1],
            recv_sem=rs_r.at[ch, r - 1],
            device_id=to_hi(r),
            device_id_type=MESH,
        )

    def gather_copy(ch, r):
        return pltpu.make_async_remote_copy(
            src_ref=gathered.at[ch, core, zhi],
            dst_ref=gathered.at[ch, core, zhi],
            send_sem=ag_s.at[ch, r - 1],
            recv_sem=ag_r.at[ch, r - 1],
            device_id=to_hi(r),
            device_id_type=MESH,
        )

    def share_copy(ch):
        return pltpu.make_async_remote_copy(
            src_ref=gathered.at[ch, core],
            dst_ref=gathered.at[ch, core],
            send_sem=sib_s.at[ch],
            recv_sem=sib_r.at[ch],
            device_id=sibling,
            device_id_type=MESH,
        )

    quarter = ROWS // 4
    for ch in range(NCH):
        def wait_return(m, carry):
            wait_bytes(returned.at[ch, m], ret_r.at[ch, m])
            return carry

        wait_bytes(returned.at[ch, 0, pl.ds(1, NLO - 1)], ret_r.at[ch, 0])
        lax.fori_loop(1, NY, wait_return, 0)
        mixed = jnp.dot(combining[...], returned[ch].reshape(slots, CW), preferred_element_type=F32)
        mixed = mixed.reshape(4, quarter, CW)
        mixed_f[ch] = mixed
        mixed_b[ch] = mixed.astype(BF16)
        for r in range(1, 4):
            scatter_copy(ch, r).start()
        for r in range(1, 4):
            scatter_copy(ch, r).wait_recv()
        total = mixed_f[ch, zhi]
        for r in range(3):
            total = total + scattered[ch, r].astype(F32)
        gathered[ch, core, zhi] = total.astype(BF16)
        for r in range(1, 4):
            gather_copy(ch, r).start()
    for ch in range(NCH):
        for r in range(1, 4):
            gather_copy(ch, r).wait()
        share_copy(ch).start()
    for ch in range(NCH):
        share_copy(ch).wait()

    blocks = [(h, ch) for h in range(2) for ch in range(NCH)]
    spans = [slice(h * HALF + ch * CW, h * HALF + (ch + 1) * CW) for h, ch in blocks]
    summed = [
        tokens[:, span].astype(F32) + gathered[ch, h].reshape(ROWS, CW).astype(F32)
        for (h, ch), span in zip(blocks, spans)
    ]
    mean = sum(jnp.sum(s, axis=1, keepdims=True) for s in summed) / D
    centered = [s - mean for s in summed]
    spread = sum(jnp.sum(s * s, axis=1, keepdims=True) for s in centered) / D
    scale = lax.rsqrt(spread + 1e-05)
    loads[2].wait()
    loads[3].wait()
    keys = values = jnp.zeros((ROWS, HEAD_DIM), F32)
    for block, span in zip(centered, spans):
        memory = (block * scale * gain[:, span] + bias[:, span]).astype(BF16)
        keys = keys + jnp.dot(memory, kw[span, :], preferred_element_type=F32)
        values = values + jnp.dot(memory, vw[span, :], preferred_element_type=F32)
    keys, values = keys.astype(BF16), values.astype(BF16)
    scores = lax.dot_general(queries[...], keys, (((1,), (1,)), ((), ())), preferred_element_type=F32)
    scores = scores * HEAD_DIM ** (-0.5)
    position = lax.broadcasted_iota(jnp.int32, (ROWS, ROWS), 1)
    scores = jnp.where(position < source_len[0], scores, -jnp.inf)
    expo = jnp.exp(scores - jnp.max(scores, axis=1, keepdims=True))
    weights = (expo / jnp.sum(expo, axis=1, keepdims=True)).astype(BF16)
    result = jnp.dot(weights, values, preferred_element_type=F32)
    row = lax.broadcasted_iota(jnp.int32, (ROWS, HEAD_DIM), 0)
    context[...] = jnp.where(row < target_len[0], result, 0.0).astype(BF16)

    wait_bytes(outgoing.at[0, pl.ds(1, NLO - 1)], disp_s.at[0])
    for ch in range(NCH):
        wait_bytes(part.at[ch, 0, pl.ds(1, NLO - 1)], ret_s.at[ch, 0])

    def drain(m, carry):
        wait_bytes(outgoing.at[m], disp_s.at[m])
        for ch in range(NCH):
            wait_bytes(part.at[ch, m], ret_s.at[ch, m])
        return carry

    lax.fori_loop(1, NY, drain, 0)

    def drain_forward(m, carry):
        wait_bytes(arrived.at[core, m], fwd_s.at[m])
        return carry

    lax.fori_loop(0, NY, drain_forward, 0)
    for ch in range(NCH):
        for r in range(1, 4):
            scatter_copy(ch, r).wait_send()


def shards(
    tokens, routes, gates, fc_in, fc_out, norm_gain, norm_bias, key_weight, value_weight, queries,
    source_len, target_len,
):
    vmem = pl.BlockSpec(memory_space=pltpu.VMEM)
    smem = pl.BlockSpec(memory_space=pltpu.SMEM)
    hbm = pl.BlockSpec(memory_space=pl.ANY)
    dma = pltpu.SemaphoreType.DMA
    return pl.pallas_call(
        kernel,
        out_shape=jax.ShapeDtypeStruct((ROWS, HEAD_DIM), BF16),
        in_specs=[vmem, vmem, vmem, hbm, hbm, vmem, vmem, hbm, hbm, vmem, smem, smem],
        out_specs=vmem,
        scratch_shapes=[
            pltpu.VMEM((NY, NLO, 2 * CAP, HALF), BF16),
            pltpu.VMEM((2, NY, NLO, 2 * CAP, HALF), BF16),
            pltpu.VMEM((2, NY * NLO * CAP, D), BF16),
            pltpu.VMEM((2, D, HID), BF16),
            pltpu.VMEM((2, 2, HID, HALF), BF16),
            pltpu.VMEM((D, HEAD_DIM), BF16),
            pltpu.VMEM((D, HEAD_DIM), BF16),
            pltpu.VMEM((2, 2, NY * NLO * CAP, HID), BF16),
            pltpu.VMEM((NCH, NY, NLO, 2 * CAP, CW), BF16),
            pltpu.VMEM((NCH, NY, NLO, 2 * CAP, CW), BF16),
            pltpu.VMEM((ROWS, NY * NLO * 2 * CAP), BF16),
            pltpu.VMEM((NCH, 4, ROWS // 4, CW), F32),
            pltpu.VMEM((NCH, 4, ROWS // 4, CW), BF16),
            pltpu.VMEM((NCH, 3, ROWS // 4, CW), BF16),
            pltpu.VMEM((NCH, 2, 4, ROWS // 4, CW), BF16),
            dma((4,)),
            dma((NY,)), dma((NY,)),
            dma((NY,)), dma((NY,)),
            dma, dma,
            dma((2,)), dma((2,)),
            dma((NCH, NY)), dma((NCH, NY)),
            dma((NCH, 3)), dma((NCH, 3)),
            dma((NCH, 3)), dma((NCH, 3)),
            dma((NCH,)), dma((NCH,)),
        ],
        compiler_params=pltpu.CompilerParams(
            collective_id=0, has_side_effects=True, vmem_limit_bytes=56 * 2**20
        ),
        cost_estimate=pl.CostEstimate(flops=2_300_000_000, bytes_accessed=10_000_000, transcendentals=20_000),
    )(
        tokens, routes, gates, fc_in, fc_out, norm_gain.reshape(1, -1), norm_bias.reshape(1, -1),
        key_weight, value_weight, queries, source_len, target_len,
    )


def solution(mesh):
    in_specs = (
        P(("dp", "expert"), None),
        P(("dp", "expert"), None),
        P(("dp", "expert"), None),
        P("expert", None, "section"),
        P("expert", "section", None),
        P(),
        P(),
        P(None, "section"),
        P(None, "section"),
        P(("dp", "expert"), "section"),
        P(("dp", "expert")),
        P(("dp", "expert")),
    )
    out_specs = P(("dp", "expert"), "section")
    return jax.shard_map(shards, mesh=mesh, in_specs=in_specs, out_specs=out_specs, check_vma=False)
```

```python
import functools

import jax
import jax.numpy as jnp
from jax import lax
from jax.experimental import pallas as pl
from jax.experimental.pallas import tpu as pltpu
from jax.sharding import PartitionSpec as P

MESH = pl.DeviceIdType.MESH
BF16, F32 = jnp.bfloat16, jnp.float32

HEAD_DIM = 128
ROWS = 128
D = 2048
HALF = 1024
HID = 512
CAP = 8
NY, NZ, NLO = 8, 16, 4
NCH, CW = 2, 512
FIRST = 5
PEERS = NY * NLO
SLOT = 2 * CAP
NEAR, FAR = 0, 1
SETS = ((0, FIRST), (FIRST, NY))
MOVED = ((1, FIRST * NLO), (FIRST * NLO, PEERS))
HOLD = 1


def dy_of(m):
    return ((m + 1) // 2) * (1 - 2 * ((m + 1) % 2))


def mirror(m):
    return jnp.where((m == 0) | (m == 7), m, m + 1 - 2 * ((m + 1) % 2))


def dz_of(d, core):
    return d - 4 * ((d + core) // 3)


def kernel(
    tokens, routes, gates, fc_in, fc_out, gain, bias, key_w, value_w, queries, source_len, target_len,
    context,
    outgoing, arrived, rows_in, w_in, w_out, kv, hidden, part, returned, combining,
    mixed_f, mixed_b, scattered, gathered,
    load_sem, disp_s, disp_r, fwd_s, fwd_r, swap_s, swap_r, hid_s, hid_r,
    ret_s, ret_r, rs_s, rs_r, ag_s, ag_r, sib_s, sib_r,
):
    section, group = lax.axis_index("section"), lax.axis_index("expert")
    zhi, core = section // 2, section % 2
    y, zlo = group // NLO, group % NLO
    z = zhi * NLO + zlo
    other = 1 - core

    def device(y2, z2, core2):
        return {"section": (z2 // NLO) * 2 + core2, "expert": y2 * NLO + z2 % NLO}

    def to(m, d):
        return device((y + dy_of(m) + NY) % NY, (z + dz_of(d, core) + NZ) % NZ, core)

    def to_hi(r):
        return device(y, (z + NLO * r) % NZ, core)

    sibling = device(y, z, other)

    loads = [
        pltpu.make_async_copy(fc_in, w_in, load_sem.at[0]),
        pltpu.make_async_copy(
            fc_out.at[:, :, pl.ds(pl.multiple_of(core * HALF, HALF), HALF)], w_out.at[core], load_sem.at[1]
        ),
        pltpu.make_async_copy(key_w, kv.at[:, 0:HEAD_DIM], load_sem.at[2]),
        pltpu.make_async_copy(value_w, kv.at[:, HEAD_DIM:2 * HEAD_DIM], load_sem.at[3]),
    ]
    for load in loads:
        load.start()

    barrier = pltpu.get_barrier_semaphore()

    def greet(k, carry):
        m, d = k // NLO, k % NLO
        source = device((y - dy_of(m) + NY) % NY, (z - dz_of(d, core) + NZ) % NZ, core)
        pl.semaphore_signal(barrier, inc=1, device_id=source, device_id_type=MESH)
        return carry

    lax.fori_loop(1, PEERS, greet, 0)
    for r in range(1, 4):
        pl.semaphore_signal(barrier, inc=1, device_id=to_hi(r), device_id_type=MESH)
    pl.semaphore_signal(barrier, inc=1, device_id=sibling, device_id_type=MESH)

    experts, slots = 2 * PEERS, PEERS * SLOT
    expert_id = lax.broadcasted_iota(jnp.int32, (experts, ROWS), 0)
    route0, route1 = routes[0:1, :], routes[1:2, :]
    hot0 = jnp.where(expert_id == route0, 1.0, 0.0)
    hot1 = jnp.where(expert_id == route1, 1.0, 0.0)
    earlier = jnp.where(
        lax.broadcasted_iota(jnp.int32, (ROWS, ROWS), 0) < lax.broadcasted_iota(jnp.int32, (ROWS, ROWS), 1),
        1.0, 0.0,
    )
    before = jnp.dot((hot0 + hot1).astype(BF16), earlier.astype(BF16), preferred_element_type=F32)
    slot0 = route0 * CAP + jnp.sum(before * hot0, axis=0, keepdims=True).astype(jnp.int32)
    slot1 = route1 * CAP + jnp.sum(before * hot1, axis=0, keepdims=True).astype(jnp.int32)

    def picks(first, count):
        row = lax.broadcasted_iota(jnp.int32, (count, ROWS), 0) + first
        m_row, d_row = row // (NLO * SLOT), (row // SLOT) % NLO
        group_row = ((y + dy_of(m_row) + NY) % NY) * NLO + (zlo + d_row) % NLO
        slot_row = group_row * SLOT + row % SLOT
        return slot0 == slot_row, slot1 == slot_row

    half = tokens[:, pl.ds(pl.multiple_of(core * HALF, HALF), HALF)]

    def place(pick0, pick1, m0, m1):
        placing = jnp.where(pick0 | pick1, 1.0, 0.0).astype(BF16)
        placed = jnp.dot(placing, half, preferred_element_type=F32).astype(BF16)
        outgoing[m0 * NLO:m1 * NLO] = placed.reshape((m1 - m0) * NLO, SLOT, HALF)

    def combine_matrix(pick0, pick1):
        gate0, gate1 = gates[0:1, :].astype(F32), gates[1:2, :].astype(F32)
        return (jnp.where(pick0, gate0, 0.0) + jnp.where(pick1, gate1, 0.0)).T.astype(BF16)

    def mirrored(k):
        m, d = k // NLO, k % NLO
        return mirror(m) * NLO + (NLO - d) % NLO

    def wait_bytes(ref, sem):
        pltpu.make_async_copy(ref, ref, sem).wait()

    def moved(ref, number):
        first, end = MOVED[number]
        return ref.at[pl.ds(first, end - first)]

    def dispatch_copy(k, number):
        return pltpu.make_async_remote_copy(
            src_ref=outgoing.at[k],
            dst_ref=arrived.at[core, mirrored(k)],
            send_sem=disp_s.at[number],
            recv_sem=disp_r.at[mirror(k // NLO)],
            device_id=to(k // NLO, k % NLO),
            device_id_type=MESH,
        )

    def send_dispatch(number):
        def send(k, carry):
            dispatch_copy(k, number).start()
            return carry

        lax.fori_loop(*MOVED[number], send, 0)

    near = picks(0, FIRST * NLO * SLOT)
    place(*near, 0, FIRST)
    pl.semaphore_wait(barrier, PEERS - 1 + 3 + 1)
    send_dispatch(NEAR)
    w_swap = pltpu.make_async_remote_copy(
        src_ref=fc_out.at[:, :, pl.ds(pl.multiple_of(other * HALF, HALF), HALF)],
        dst_ref=w_out.at[core],
        send_sem=swap_s,
        recv_sem=swap_r,
        device_id=sibling,
        device_id_type=MESH,
    )
    w_swap.start()
    arrived[core, 0] = outgoing[0]
    far = picks(FIRST * NLO * SLOT, (NY - FIRST) * NLO * SLOT)
    place(*far, FIRST, NY)
    wait_bytes(moved(outgoing, NEAR), disp_s.at[NEAR])
    send_dispatch(FAR)
    combining[:, :FIRST * NLO * SLOT] = combine_matrix(*near)
    combining[:, FIRST * NLO * SLOT:] = combine_matrix(*far)

    def forward_copy(m):
        blocks = pl.ds(m * NLO, NLO)
        return pltpu.make_async_remote_copy(
            src_ref=arrived.at[core, blocks],
            dst_ref=arrived.at[core, blocks],
            send_sem=fwd_s.at[m],
            recv_sem=fwd_r.at[m],
            device_id=sibling,
            device_id_type=MESH,
        )

    def hidden_copy(number):
        m0, m1 = SETS[number]
        rows = pl.ds(m0 * NLO * CAP, (m1 - m0) * NLO * CAP)
        return pltpu.make_async_remote_copy(
            src_ref=hidden.at[core, :, rows],
            dst_ref=hidden.at[core, :, rows],
            send_sem=hid_s.at[number],
            recv_sem=hid_r.at[number],
            device_id=sibling,
            device_id_type=MESH,
        )

    def make_hidden(number):
        m0, m1 = SETS[number]

        def take(m, carry):
            wait_bytes(arrived.at[core, pl.ds(m * NLO, NLO)], disp_r.at[m])
            forward_copy(m).start()
            return carry

        if m0 == 0:
            wait_bytes(arrived.at[core, pl.ds(1, NLO - 1)], disp_r.at[0])
            forward_copy(0).start()
        lax.fori_loop(max(m0, 1), m1, take, 0)

        def relayout(m, carry):
            wait_bytes(arrived.at[other, pl.ds(m * NLO, NLO)], fwd_r.at[m])
            for h in range(2):
                block = arrived[h, pl.ds(m * NLO, NLO)].astype(F32)
                for i in range(2):
                    rows_in[i, pl.ds(pl.multiple_of(m * NLO * CAP, NLO * CAP), NLO * CAP), h * HALF:(h + 1) * HALF] = (
                        block[:, i * CAP:(i + 1) * CAP, :].reshape(NLO * CAP, HALF).astype(BF16)
                    )
            return carry

        lax.fori_loop(m0, m1, relayout, 0)
        rows = slice(m0 * NLO * CAP, m1 * NLO * CAP)
        if number == NEAR:
            loads[0].wait()
        for i in range(2):
            for n in range(0, HID, 256):
                h = jnp.dot(rows_in[i, rows, :], w_in[i, :, n:n + 256], preferred_element_type=F32)
                hidden[core, i, rows, n:n + 256] = jnp.maximum(h, 0.0).astype(BF16)
        hidden_copy(number).start()
        if number == NEAR:
            loads[1].wait()
            w_swap.wait()
        hidden_copy(number).wait()

    def expert_outputs(m0, m1, ch):
        rows, cols = slice(m0 * NLO * CAP, m1 * NLO * CAP), slice(ch * CW, (ch + 1) * CW)
        sums = [
            jnp.dot(hidden[0, i, rows, :], w_out[0, i, :, cols], preferred_element_type=F32)
            + jnp.dot(hidden[1, i, rows, :], w_out[1, i, :, cols], preferred_element_type=F32)
            for i in range(2)
        ]
        sums = [s.reshape((m1 - m0) * NLO, CAP, CW) for s in sums]
        return jnp.concatenate(sums, axis=1).astype(BF16)

    def return_copy(ch, k, number):
        return pltpu.make_async_remote_copy(
            src_ref=part.at[ch, k],
            dst_ref=returned.at[ch, mirrored(k)],
            send_sem=ret_s.at[ch, number],
            recv_sem=ret_r.at[ch, number],
            device_id=to(k // NLO, k % NLO),
            device_id_type=MESH,
        )

    units = []

    def settle(left):
        while len(units) > left:
            ch, number = units.pop(0)
            wait_bytes(moved(part.at[ch], number), ret_s.at[ch, number])

    def send_back(ch, number):
        m0, m1 = SETS[number]
        part[ch, m0 * NLO:m1 * NLO] = expert_outputs(m0, m1, ch)
        settle(HOLD - 1)

        def send(k, carry):
            return_copy(ch, k, number).start()
            return carry

        lax.fori_loop(*MOVED[number], send, 0)
        units.append((ch, number))
        if number == NEAR:
            returned[ch, 0] = part[ch, 0]

    def scatter_copy(ch, r):
        return pltpu.make_async_remote_copy(
            src_ref=mixed_b.at[ch, (zhi + r) % 4],
            dst_ref=scattered.at[ch, r - 1],
            send_sem=rs_s.at[ch, r - 1],
            recv_sem=rs_r.at[ch, r - 1],
            device_id=to_hi(r),
            device_id_type=MESH,
        )

    def gather_copy(ch, r):
        return pltpu.make_async_remote_copy(
            src_ref=gathered.at[ch, core, zhi],
            dst_ref=gathered.at[ch, core, zhi],
            send_sem=ag_s.at[ch, r - 1],
            recv_sem=ag_r.at[ch, r - 1],
            device_id=to_hi(r),
            device_id_type=MESH,
        )

    def share_copy(ch):
        return pltpu.make_async_remote_copy(
            src_ref=gathered.at[ch, core],
            dst_ref=gathered.at[ch, core],
            send_sem=sib_s.at[ch],
            recv_sem=sib_r.at[ch],
            device_id=sibling,
            device_id_type=MESH,
        )

    quarter = ROWS // 4

    def scatter(ch):
        for number in (FAR, NEAR):
            wait_bytes(moved(returned.at[ch], number), ret_r.at[ch, number])
        mixed = jnp.dot(combining[...], returned[ch].reshape(slots, CW), preferred_element_type=F32)
        mixed = mixed.reshape(4, quarter, CW)
        mixed_f[ch] = mixed
        mixed_b[ch] = mixed.astype(BF16)
        for r in (2, 1, 3):
            scatter_copy(ch, r).start()

    def gather(ch):
        for r in range(1, 4):
            scatter_copy(ch, r).wait_recv()
        total = mixed_f[ch, zhi]
        for r in range(3):
            total = total + scattered[ch, r].astype(F32)
        gathered[ch, core, zhi] = total.astype(BF16)
        for r in (2, 1, 3):
            gather_copy(ch, r).start()

    def share(ch):
        for r in range(1, 4):
            gather_copy(ch, r).wait()
        share_copy(ch).start()

    make_hidden(NEAR)
    wait_bytes(moved(outgoing, FAR), disp_s.at[FAR])
    send_back(0, NEAR)
    make_hidden(FAR)
    send_back(0, FAR)
    send_back(1, NEAR)
    scatter(0)
    send_back(1, FAR)
    gather(0)
    scatter(1)
    share(0)
    gather(1)
    share(1)
    settle(0)
    for ch in range(NCH):
        share_copy(ch).wait()

    blocks = [(h, ch) for h in range(2) for ch in range(NCH)]
    spans = [slice(h * HALF + ch * CW, h * HALF + (ch + 1) * CW) for h, ch in blocks]
    summed = [
        tokens[:, span].astype(F32) + gathered[ch, h].reshape(ROWS, CW).astype(F32)
        for (h, ch), span in zip(blocks, spans)
    ]
    mean = sum(jnp.sum(s, axis=1, keepdims=True) for s in summed) / D
    centered = [s - mean for s in summed]
    spread = sum(jnp.sum(s * s, axis=1, keepdims=True) for s in centered) / D
    scale = lax.rsqrt(spread + 1e-05)
    loads[2].wait()
    loads[3].wait()
    both = jnp.zeros((ROWS, 2 * HEAD_DIM), F32)
    for block, span in zip(centered, spans):
        memory = (block * scale * gain[:, span] + bias[:, span]).astype(BF16)
        both = both + jnp.dot(memory, kv[span, :], preferred_element_type=F32)
    keys, values = both[:, :HEAD_DIM].astype(BF16), both[:, HEAD_DIM:].astype(BF16)
    scores = lax.dot_general(queries[...], keys, (((1,), (1,)), ((), ())), preferred_element_type=F32)
    scores = scores * HEAD_DIM ** (-0.5)
    position = lax.broadcasted_iota(jnp.int32, (ROWS, ROWS), 1)
    scores = jnp.where(position < source_len[0], scores, -jnp.inf)
    expo = jnp.exp(scores - jnp.max(scores, axis=1, keepdims=True))
    weights = (expo / jnp.sum(expo, axis=1, keepdims=True)).astype(BF16)
    result = jnp.dot(weights, values, preferred_element_type=F32)
    row = lax.broadcasted_iota(jnp.int32, (ROWS, HEAD_DIM), 0)
    context[...] = jnp.where(row < target_len[0], result, 0.0).astype(BF16)

    def drain_forward(m, carry):
        wait_bytes(arrived.at[core, pl.ds(m * NLO, NLO)], fwd_s.at[m])
        return carry

    lax.fori_loop(0, NY, drain_forward, 0)
    for ch in range(NCH):
        for r in range(1, 4):
            scatter_copy(ch, r).wait_send()


def shards(
    tokens, routes, gates, fc_in, fc_out, norm_gain, norm_bias, key_weight, value_weight, queries,
    source_len, target_len,
):
    vmem = pl.BlockSpec(memory_space=pltpu.VMEM)
    smem = pl.BlockSpec(memory_space=pltpu.SMEM)
    hbm = pl.BlockSpec(memory_space=pl.ANY)
    dma = pltpu.SemaphoreType.DMA
    return pl.pallas_call(
        kernel,
        out_shape=jax.ShapeDtypeStruct((ROWS, HEAD_DIM), BF16),
        in_specs=[vmem, vmem, vmem, hbm, hbm, vmem, vmem, hbm, hbm, vmem, smem, smem],
        out_specs=vmem,
        scratch_shapes=[
            pltpu.VMEM((PEERS, SLOT, HALF), BF16),
            pltpu.VMEM((2, PEERS, SLOT, HALF), BF16),
            pltpu.VMEM((2, PEERS * CAP, D), BF16),
            pltpu.VMEM((2, D, HID), BF16),
            pltpu.VMEM((2, 2, HID, HALF), BF16),
            pltpu.VMEM((D, 2 * HEAD_DIM), BF16),
            pltpu.VMEM((2, 2, PEERS * CAP, HID), BF16),
            pltpu.VMEM((NCH, PEERS, SLOT, CW), BF16),
            pltpu.VMEM((NCH, PEERS, SLOT, CW), BF16),
            pltpu.VMEM((ROWS, PEERS * SLOT), BF16),
            pltpu.VMEM((NCH, 4, ROWS // 4, CW), F32),
            pltpu.VMEM((NCH, 4, ROWS // 4, CW), BF16),
            pltpu.VMEM((NCH, 3, ROWS // 4, CW), BF16),
            pltpu.VMEM((NCH, 2, 4, ROWS // 4, CW), BF16),
            dma((4,)),
            dma((2,)), dma((NY,)),
            dma((NY,)), dma((NY,)),
            dma, dma,
            dma((2,)), dma((2,)),
            dma((NCH, 2)), dma((NCH, 2)),
            dma((NCH, 3)), dma((NCH, 3)),
            dma((NCH, 3)), dma((NCH, 3)),
            dma((NCH,)), dma((NCH,)),
        ],
        compiler_params=pltpu.CompilerParams(
            collective_id=0, has_side_effects=True, vmem_limit_bytes=56 * 2**20
        ),
        cost_estimate=pl.CostEstimate(flops=2_300_000_000, bytes_accessed=10_000_000, transcendentals=20_000),
    )(
        tokens, routes.T, gates.T, fc_in, fc_out, norm_gain.reshape(1, -1), norm_bias.reshape(1, -1),
        key_weight, value_weight, queries, source_len, target_len,
    )


def solution(mesh):
    in_specs = (
        P(("dp", "expert"), None),
        P(("dp", "expert"), None),
        P(("dp", "expert"), None),
        P("expert", None, "section"),
        P("expert", "section", None),
        P(),
        P(),
        P(None, "section"),
        P(None, "section"),
        P(("dp", "expert"), "section"),
        P(("dp", "expert")),
        P(("dp", "expert")),
    )
    out_specs = P(("dp", "expert"), "section")
    return jax.shard_map(shards, mesh=mesh, in_specs=in_specs, out_specs=out_specs, check_vma=False)
```

```python
import functools

import jax
import jax.numpy as jnp
from jax import lax
from jax.experimental import pallas as pl
from jax.experimental.pallas import tpu as pltpu
from jax.sharding import PartitionSpec as P

MESH = pl.DeviceIdType.MESH
BF16, F32 = jnp.bfloat16, jnp.float32

HEAD_DIM = 128
ROWS = 128
D = 2048
HALF = 1024
HID = 512
CAP = 8
NY, NZ, NLO = 8, 16, 4
NCH, CW = 2, 512
FIRST = 5
PEERS = NY * NLO
SLOT = 2 * CAP
NEAR, FAR = 0, 1
SETS = ((0, FIRST), (FIRST, NY))
MOVED = ((1, FIRST * NLO), (FIRST * NLO, PEERS))
HOLD = 1


def dy_of(m):
    return ((m + 1) // 2) * (1 - 2 * ((m + 1) % 2))


def mirror(m):
    return jnp.where((m == 0) | (m == 7), m, m + 1 - 2 * ((m + 1) % 2))


def dz_of(d, core):
    return d - 4 * ((d + core) // 3)


def kernel(
    tokens_h, routes, gates, fc_in, fc_out, gain_h, bias_h, key_w, value_w, queries_h, source_len, target_len,
    context,
    tokens, gain, bias, queries,
    outgoing, arrived, rows_in, w_in, w_out, kv, hidden, part, returned, combining,
    mixed_f, mixed_b, scattered, gathered,
    load_sem, disp_s, disp_r, fwd_s, fwd_r, swap_s, swap_r, hid_s, hid_r,
    ret_s, ret_r, rs_s, rs_r, ag_s, ag_r, sib_s, sib_r,
):
    section, group = lax.axis_index("section"), lax.axis_index("expert")
    zhi, core = section // 2, section % 2
    y, zlo = group // NLO, group % NLO
    z = zhi * NLO + zlo
    other = 1 - core

    def device(y2, z2, core2):
        return {"section": (z2 // NLO) * 2 + core2, "expert": y2 * NLO + z2 % NLO}

    def to(m, d):
        return device((y + dy_of(m) + NY) % NY, (z + dz_of(d, core) + NZ) % NZ, core)

    def to_hi(r):
        return device(y, (z + NLO * r) % NZ, core)

    sibling = device(y, z, other)

    tokens_load = pltpu.make_async_copy(tokens_h, tokens, load_sem.at[4])
    tokens_load.start()
    loads = [
        pltpu.make_async_copy(fc_in, w_in.at[core], load_sem.at[0]),
        pltpu.make_async_copy(
            fc_out.at[:, :, pl.ds(pl.multiple_of(core * HALF, HALF), HALF)], w_out.at[core], load_sem.at[1]
        ),
        pltpu.make_async_copy(key_w, kv.at[:, 0:HEAD_DIM], load_sem.at[2]),
        pltpu.make_async_copy(value_w, kv.at[:, HEAD_DIM:2 * HEAD_DIM], load_sem.at[3]),
        pltpu.make_async_copy(gain_h, gain, load_sem.at[5]),
        pltpu.make_async_copy(bias_h, bias, load_sem.at[6]),
        pltpu.make_async_copy(queries_h, queries, load_sem.at[7]),
    ]

    barrier = pltpu.get_barrier_semaphore()

    def greet(k, carry):
        m, d = k // NLO, k % NLO
        source = device((y - dy_of(m) + NY) % NY, (z - dz_of(d, core) + NZ) % NZ, core)
        pl.semaphore_signal(barrier, inc=1, device_id=source, device_id_type=MESH)
        return carry

    lax.fori_loop(1, PEERS, greet, 0)
    for r in range(1, 4):
        pl.semaphore_signal(barrier, inc=1, device_id=to_hi(r), device_id_type=MESH)
    pl.semaphore_signal(barrier, inc=1, device_id=sibling, device_id_type=MESH)

    experts, slots = 2 * PEERS, PEERS * SLOT
    expert_id = lax.broadcasted_iota(jnp.int32, (experts, ROWS), 0)
    route0, route1 = routes[0:1, :], routes[1:2, :]
    hot0 = jnp.where(expert_id == route0, 1.0, 0.0)
    hot1 = jnp.where(expert_id == route1, 1.0, 0.0)
    earlier = jnp.where(
        lax.broadcasted_iota(jnp.int32, (ROWS, ROWS), 0) < lax.broadcasted_iota(jnp.int32, (ROWS, ROWS), 1),
        1.0, 0.0,
    )
    before = jnp.dot((hot0 + hot1).astype(BF16), earlier.astype(BF16), preferred_element_type=F32)
    slot0 = route0 * CAP + jnp.sum(before * hot0, axis=0, keepdims=True).astype(jnp.int32)
    slot1 = route1 * CAP + jnp.sum(before * hot1, axis=0, keepdims=True).astype(jnp.int32)

    def picks(first, count):
        row = lax.broadcasted_iota(jnp.int32, (count, ROWS), 0) + first
        m_row, d_row = row // (NLO * SLOT), (row // SLOT) % NLO
        group_row = ((y + dy_of(m_row) + NY) % NY) * NLO + (zlo + d_row) % NLO
        slot_row = group_row * SLOT + row % SLOT
        return slot0 == slot_row, slot1 == slot_row

    for load in loads:
        load.start()
    tokens_load.wait()
    half = tokens[:, pl.ds(pl.multiple_of(core * HALF, HALF), HALF)]

    def place(pick0, pick1, m0, m1):
        placing = jnp.where(pick0 | pick1, 1.0, 0.0).astype(BF16)
        placed = jnp.dot(placing, half, preferred_element_type=F32).astype(BF16)
        outgoing[m0 * NLO:m1 * NLO] = placed.reshape((m1 - m0) * NLO, SLOT, HALF)

    def combine_matrix(pick0, pick1):
        gate0, gate1 = gates[0:1, :].astype(F32), gates[1:2, :].astype(F32)
        return (jnp.where(pick0, gate0, 0.0) + jnp.where(pick1, gate1, 0.0)).T.astype(BF16)

    def mirrored(k):
        m, d = k // NLO, k % NLO
        return mirror(m) * NLO + (NLO - d) % NLO

    def wait_bytes(ref, sem):
        pltpu.make_async_copy(ref, ref, sem).wait()

    def moved(ref, number):
        first, end = MOVED[number]
        return ref.at[pl.ds(first, end - first)]

    def dispatch_copy(k, number):
        return pltpu.make_async_remote_copy(
            src_ref=outgoing.at[k],
            dst_ref=arrived.at[core, mirrored(k)],
            send_sem=disp_s.at[number],
            recv_sem=disp_r.at[mirror(k // NLO)],
            device_id=to(k // NLO, k % NLO),
            device_id_type=MESH,
        )

    def send_dispatch(number):
        def send(k, carry):
            dispatch_copy(k, number).start()
            return carry

        lax.fori_loop(*MOVED[number], send, 0)

    near = picks(0, FIRST * NLO * SLOT)
    place(*near, 0, FIRST)
    pl.semaphore_wait(barrier, PEERS - 1 + 3 + 1)
    send_dispatch(NEAR)
    w_swap = pltpu.make_async_remote_copy(
        src_ref=fc_out.at[:, :, pl.ds(pl.multiple_of(other * HALF, HALF), HALF)],
        dst_ref=w_out.at[core],
        send_sem=swap_s,
        recv_sem=swap_r,
        device_id=sibling,
        device_id_type=MESH,
    )
    in_swap = pltpu.make_async_remote_copy(
        src_ref=fc_in,
        dst_ref=w_in.at[core],
        send_sem=hid_s,
        recv_sem=hid_r,
        device_id=sibling,
        device_id_type=MESH,
    )
    in_swap.start()
    w_swap.start()
    arrived[core, 0] = outgoing[0]
    far = picks(FIRST * NLO * SLOT, (NY - FIRST) * NLO * SLOT)
    place(*far, FIRST, NY)
    wait_bytes(moved(outgoing, NEAR), disp_s.at[NEAR])
    send_dispatch(FAR)
    combining[:, :FIRST * NLO * SLOT] = combine_matrix(*near)
    combining[:, FIRST * NLO * SLOT:] = combine_matrix(*far)

    def forward_copy(m):
        blocks = pl.ds(m * NLO, NLO)
        return pltpu.make_async_remote_copy(
            src_ref=arrived.at[core, blocks],
            dst_ref=arrived.at[core, blocks],
            send_sem=fwd_s.at[m],
            recv_sem=fwd_r.at[m],
            device_id=sibling,
            device_id_type=MESH,
        )

    def make_hidden(number):
        m0, m1 = SETS[number]

        def take(m, carry):
            wait_bytes(arrived.at[core, pl.ds(m * NLO, NLO)], disp_r.at[m])
            forward_copy(m).start()
            return carry

        if m0 == 0:
            wait_bytes(arrived.at[core, pl.ds(1, NLO - 1)], disp_r.at[0])
            forward_copy(0).start()
        lax.fori_loop(max(m0, 1), m1, take, 0)

        def relayout(m, carry):
            wait_bytes(arrived.at[other, pl.ds(m * NLO, NLO)], fwd_r.at[m])
            for h in range(2):
                block = arrived[h, pl.ds(m * NLO, NLO)].astype(F32)
                for i in range(2):
                    rows_in[i, pl.ds(pl.multiple_of(m * NLO * CAP, NLO * CAP), NLO * CAP), h * HALF:(h + 1) * HALF] = (
                        block[:, i * CAP:(i + 1) * CAP, :].reshape(NLO * CAP, HALF).astype(BF16)
                    )
            return carry

        lax.fori_loop(m0, m1, relayout, 0)
        rows = slice(m0 * NLO * CAP, m1 * NLO * CAP)
        if number == NEAR:
            loads[0].wait()
            in_swap.wait()
        for sec in range(2):
            for i in range(2):
                for n in range(0, HID, 256):
                    h = jnp.dot(rows_in[i, rows, :], w_in[sec, i, :, n:n + 256], preferred_element_type=F32)
                    hidden[sec, i, rows, n:n + 256] = jnp.maximum(h, 0.0).astype(BF16)
        if number == NEAR:
            loads[1].wait()
            w_swap.wait()

    def expert_outputs(m0, m1, ch):
        rows, cols = slice(m0 * NLO * CAP, m1 * NLO * CAP), slice(ch * CW, (ch + 1) * CW)
        sums = [
            jnp.dot(hidden[0, i, rows, :], w_out[0, i, :, cols], preferred_element_type=F32)
            + jnp.dot(hidden[1, i, rows, :], w_out[1, i, :, cols], preferred_element_type=F32)
            for i in range(2)
        ]
        sums = [s.reshape((m1 - m0) * NLO, CAP, CW) for s in sums]
        return jnp.concatenate(sums, axis=1).astype(BF16)

    def return_copy(ch, k, number):
        return pltpu.make_async_remote_copy(
            src_ref=part.at[ch, k],
            dst_ref=returned.at[ch, mirrored(k)],
            send_sem=ret_s.at[ch, number],
            recv_sem=ret_r.at[ch, number],
            device_id=to(k // NLO, k % NLO),
            device_id_type=MESH,
        )

    units = []

    def settle(left):
        while len(units) > left:
            ch, number = units.pop(0)
            wait_bytes(moved(part.at[ch], number), ret_s.at[ch, number])

    def send_back(ch, number):
        m0, m1 = SETS[number]
        part[ch, m0 * NLO:m1 * NLO] = expert_outputs(m0, m1, ch)
        settle(HOLD - 1)

        def send(k, carry):
            return_copy(ch, k, number).start()
            return carry

        lax.fori_loop(*MOVED[number], send, 0)
        units.append((ch, number))
        if number == NEAR:
            returned[ch, 0] = part[ch, 0]

    def scatter_copy(ch, r):
        return pltpu.make_async_remote_copy(
            src_ref=mixed_b.at[ch, (zhi + r) % 4],
            dst_ref=scattered.at[ch, r - 1],
            send_sem=rs_s.at[ch, r - 1],
            recv_sem=rs_r.at[ch, r - 1],
            device_id=to_hi(r),
            device_id_type=MESH,
        )

    def gather_copy(ch, r):
        return pltpu.make_async_remote_copy(
            src_ref=gathered.at[ch, core, zhi],
            dst_ref=gathered.at[ch, core, zhi],
            send_sem=ag_s.at[ch, r - 1],
            recv_sem=ag_r.at[ch, r - 1],
            device_id=to_hi(r),
            device_id_type=MESH,
        )

    def share_copy(ch):
        return pltpu.make_async_remote_copy(
            src_ref=gathered.at[ch, core],
            dst_ref=gathered.at[ch, core],
            send_sem=sib_s.at[ch],
            recv_sem=sib_r.at[ch],
            device_id=sibling,
            device_id_type=MESH,
        )

    quarter = ROWS // 4

    def scatter(ch):
        for number in (FAR, NEAR):
            wait_bytes(moved(returned.at[ch], number), ret_r.at[ch, number])
        mixed = jnp.dot(combining[...], returned[ch].reshape(slots, CW), preferred_element_type=F32)
        mixed = mixed.reshape(4, quarter, CW)
        mixed_f[ch] = mixed
        mixed_b[ch] = mixed.astype(BF16)
        for r in (2, 1, 3):
            scatter_copy(ch, r).start()

    def gather(ch):
        for r in range(1, 4):
            scatter_copy(ch, r).wait_recv()
        total = mixed_f[ch, zhi]
        for r in range(3):
            total = total + scattered[ch, r].astype(F32)
        gathered[ch, core, zhi] = total.astype(BF16)
        for r in (2, 1, 3):
            gather_copy(ch, r).start()

    def share(ch):
        for r in range(1, 4):
            gather_copy(ch, r).wait()
        share_copy(ch).start()

    make_hidden(NEAR)
    wait_bytes(moved(outgoing, FAR), disp_s.at[FAR])
    send_back(0, NEAR)
    make_hidden(FAR)
    send_back(0, FAR)
    send_back(1, NEAR)
    scatter(0)
    send_back(1, FAR)
    gather(0)
    scatter(1)
    share(0)
    gather(1)
    share(1)
    settle(0)
    for ch in range(NCH):
        share_copy(ch).wait()

    blocks = [(h, ch) for h in range(2) for ch in range(NCH)]
    spans = [slice(h * HALF + ch * CW, h * HALF + (ch + 1) * CW) for h, ch in blocks]
    summed = [
        tokens[:, span].astype(F32) + gathered[ch, h].reshape(ROWS, CW).astype(F32)
        for (h, ch), span in zip(blocks, spans)
    ]
    mean = sum(jnp.sum(s, axis=1, keepdims=True) for s in summed) / D
    centered = [s - mean for s in summed]
    spread = sum(jnp.sum(s * s, axis=1, keepdims=True) for s in centered) / D
    scale = lax.rsqrt(spread + 1e-05)
    for load in loads[2:]:
        load.wait()
    both = jnp.zeros((ROWS, 2 * HEAD_DIM), F32)
    for block, span in zip(centered, spans):
        memory = (block * scale * gain[:, span] + bias[:, span]).astype(BF16)
        both = both + jnp.dot(memory, kv[span, :], preferred_element_type=F32)
    keys, values = both[:, :HEAD_DIM].astype(BF16), both[:, HEAD_DIM:].astype(BF16)
    scores = lax.dot_general(queries[...], keys, (((1,), (1,)), ((), ())), preferred_element_type=F32)
    scores = scores * HEAD_DIM ** (-0.5)
    position = lax.broadcasted_iota(jnp.int32, (ROWS, ROWS), 1)
    scores = jnp.where(position < source_len[0], scores, -jnp.inf)
    expo = jnp.exp(scores - jnp.max(scores, axis=1, keepdims=True))
    weights = (expo / jnp.sum(expo, axis=1, keepdims=True)).astype(BF16)
    result = jnp.dot(weights, values, preferred_element_type=F32)
    row = lax.broadcasted_iota(jnp.int32, (ROWS, HEAD_DIM), 0)
    context[...] = jnp.where(row < target_len[0], result, 0.0).astype(BF16)

    def drain_forward(m, carry):
        wait_bytes(arrived.at[core, pl.ds(m * NLO, NLO)], fwd_s.at[m])
        return carry

    lax.fori_loop(0, NY, drain_forward, 0)
    for ch in range(NCH):
        for r in range(1, 4):
            scatter_copy(ch, r).wait_send()


def shards(
    tokens, routes, gates, fc_in, fc_out, norm_gain, norm_bias, key_weight, value_weight, queries,
    source_len, target_len,
):
    vmem = pl.BlockSpec(memory_space=pltpu.VMEM)
    smem = pl.BlockSpec(memory_space=pltpu.SMEM)
    hbm = pl.BlockSpec(memory_space=pl.ANY)
    dma = pltpu.SemaphoreType.DMA
    return pl.pallas_call(
        kernel,
        out_shape=jax.ShapeDtypeStruct((ROWS, HEAD_DIM), BF16),
        in_specs=[hbm, vmem, vmem, hbm, hbm, hbm, hbm, hbm, hbm, hbm, smem, smem],
        out_specs=vmem,
        scratch_shapes=[
            pltpu.VMEM((ROWS, D), BF16),
            pltpu.VMEM((1, D), F32),
            pltpu.VMEM((1, D), F32),
            pltpu.VMEM((ROWS, HEAD_DIM), BF16),
            pltpu.VMEM((PEERS, SLOT, HALF), BF16),
            pltpu.VMEM((2, PEERS, SLOT, HALF), BF16),
            pltpu.VMEM((2, PEERS * CAP, D), BF16),
            pltpu.VMEM((2, 2, D, HID), BF16),
            pltpu.VMEM((2, 2, HID, HALF), BF16),
            pltpu.VMEM((D, 2 * HEAD_DIM), BF16),
            pltpu.VMEM((2, 2, PEERS * CAP, HID), BF16),
            pltpu.VMEM((NCH, PEERS, SLOT, CW), BF16),
            pltpu.VMEM((NCH, PEERS, SLOT, CW), BF16),
            pltpu.VMEM((ROWS, PEERS * SLOT), BF16),
            pltpu.VMEM((NCH, 4, ROWS // 4, CW), F32),
            pltpu.VMEM((NCH, 4, ROWS // 4, CW), BF16),
            pltpu.VMEM((NCH, 3, ROWS // 4, CW), BF16),
            pltpu.VMEM((NCH, 2, 4, ROWS // 4, CW), BF16),
            dma((8,)),
            dma((2,)), dma((NY,)),
            dma((NY,)), dma((NY,)),
            dma, dma,
            dma, dma,
            dma((NCH, 2)), dma((NCH, 2)),
            dma((NCH, 3)), dma((NCH, 3)),
            dma((NCH, 3)), dma((NCH, 3)),
            dma((NCH,)), dma((NCH,)),
        ],
        compiler_params=pltpu.CompilerParams(
            collective_id=0, has_side_effects=True, vmem_limit_bytes=56 * 2**20
        ),
        cost_estimate=pl.CostEstimate(flops=2_300_000_000, bytes_accessed=10_000_000, transcendentals=20_000),
    )(
        tokens, routes.T, gates.T, fc_in, fc_out, norm_gain.reshape(1, -1), norm_bias.reshape(1, -1),
        key_weight, value_weight, queries, source_len, target_len,
    )


def solution(mesh):
    in_specs = (
        P(("dp", "expert"), None),
        P(("dp", "expert"), None),
        P(("dp", "expert"), None),
        P("expert", None, "section"),
        P("expert", "section", None),
        P(),
        P(),
        P(None, "section"),
        P(None, "section"),
        P(("dp", "expert"), "section"),
        P(("dp", "expert")),
        P(("dp", "expert")),
    )
    out_specs = P(("dp", "expert"), "section")
    return jax.shard_map(shards, mesh=mesh, in_specs=in_specs, out_specs=out_specs, check_vma=False)
```

```python
import functools

import jax
import jax.numpy as jnp
from jax import lax
from jax.experimental import pallas as pl
from jax.experimental.pallas import tpu as pltpu
from jax.sharding import PartitionSpec as P

MESH = pl.DeviceIdType.MESH
BF16, F32 = jnp.bfloat16, jnp.float32

HEAD_DIM = 128
ROWS = 128
D = 2048
HALF = 1024
HID = 512
CAP = 8
NY, NZ, NLO = 8, 16, 4
NCH, CW = 2, 512
FIRST = 5
PEERS = NY * NLO
SLOT = 2 * CAP
NEAR, FAR = 0, 1
SETS = ((0, FIRST), (FIRST, NY))
MOVED = ((1, FIRST * NLO), (FIRST * NLO, PEERS))
HOLD = 1


def dy_of(m):
    return ((m + 1) // 2) * (1 - 2 * ((m + 1) % 2))


def mirror(m):
    return jnp.where((m == 0) | (m == 7), m, m + 1 - 2 * ((m + 1) % 2))


def dz_of(d, core):
    return d - 4 * ((d + core) // 3)


def kernel(
    tokens_h, routes, gates, fc_in, fc_out, gain_h, bias_h, key_w, value_w, queries_h, source_len, target_len,
    context,
    tokens, gain, bias, queries,
    outgoing, arrived, rows_in, w_in, w_out, kv, hidden, part, returned, combining,
    mixed_f, mixed_b, scattered, gathered,
    load_sem, disp_s, disp_r, fwd_s, fwd_r, swap_s, swap_r, hid_s, hid_r,
    ret_s, ret_r, rs_s, rs_r, ag_s, ag_r, sib_s, sib_r,
):
    section, group = lax.axis_index("section"), lax.axis_index("expert")
    zhi, core = section // 2, section % 2
    y, zlo = group // NLO, group % NLO
    z = zhi * NLO + zlo
    other = 1 - core

    def device(y2, z2, core2):
        return {"section": (z2 // NLO) * 2 + core2, "expert": y2 * NLO + z2 % NLO}

    def to(m, d):
        return device((y + dy_of(m) + NY) % NY, (z + dz_of(d, core) + NZ) % NZ, core)

    def to_hi(r):
        return device(y, (z + NLO * r) % NZ, core)

    sibling = device(y, z, other)

    tokens_load = pltpu.make_async_copy(tokens_h, tokens, load_sem.at[4])
    tokens_load.start()
    loads = [
        pltpu.make_async_copy(fc_in, w_in.at[core], load_sem.at[0]),
        pltpu.make_async_copy(
            fc_out.at[:, :, pl.ds(pl.multiple_of(core * HALF, HALF), HALF)], w_out.at[core], load_sem.at[1]
        ),
        pltpu.make_async_copy(key_w, kv.at[:, 0:HEAD_DIM], load_sem.at[2]),
        pltpu.make_async_copy(value_w, kv.at[:, HEAD_DIM:2 * HEAD_DIM], load_sem.at[3]),
        pltpu.make_async_copy(gain_h, gain, load_sem.at[5]),
        pltpu.make_async_copy(bias_h, bias, load_sem.at[6]),
        pltpu.make_async_copy(queries_h, queries, load_sem.at[7]),
    ]

    barrier = pltpu.get_barrier_semaphore()

    def greet(k, carry):
        m, d = k // NLO, k % NLO
        source = device((y - dy_of(m) + NY) % NY, (z - dz_of(d, core) + NZ) % NZ, core)
        pl.semaphore_signal(barrier, inc=1, device_id=source, device_id_type=MESH)
        return carry

    lax.fori_loop(1, PEERS, greet, 0)
    for r in range(1, 4):
        pl.semaphore_signal(barrier, inc=1, device_id=to_hi(r), device_id_type=MESH)
    pl.semaphore_signal(barrier, inc=1, device_id=sibling, device_id_type=MESH)

    experts, slots = 2 * PEERS, PEERS * SLOT
    expert_id = lax.broadcasted_iota(jnp.int32, (experts, ROWS), 0)
    route0, route1 = routes[0:1, :], routes[1:2, :]
    hot0 = jnp.where(expert_id == route0, 1.0, 0.0)
    hot1 = jnp.where(expert_id == route1, 1.0, 0.0)
    earlier = jnp.where(
        lax.broadcasted_iota(jnp.int32, (ROWS, ROWS), 0) < lax.broadcasted_iota(jnp.int32, (ROWS, ROWS), 1),
        1.0, 0.0,
    )
    before = jnp.dot((hot0 + hot1).astype(BF16), earlier.astype(BF16), preferred_element_type=F32)
    slot0 = route0 * CAP + jnp.sum(before * hot0, axis=0, keepdims=True).astype(jnp.int32)
    slot1 = route1 * CAP + jnp.sum(before * hot1, axis=0, keepdims=True).astype(jnp.int32)

    def picks(first, count):
        row = lax.broadcasted_iota(jnp.int32, (count, ROWS), 0) + first
        m_row, d_row = row // (NLO * SLOT), (row // SLOT) % NLO
        group_row = ((y + dy_of(m_row) + NY) % NY) * NLO + (zlo + d_row) % NLO
        slot_row = group_row * SLOT + row % SLOT
        return slot0 == slot_row, slot1 == slot_row

    for load in loads:
        load.start()
    tokens_load.wait()
    half = tokens[:, pl.ds(pl.multiple_of(core * HALF, HALF), HALF)]

    def place(pick0, pick1, m0, m1):
        placing = jnp.where(pick0 | pick1, 1.0, 0.0).astype(BF16)
        placed = jnp.dot(placing, half, preferred_element_type=F32).astype(BF16)
        outgoing[m0 * NLO:m1 * NLO] = placed.reshape((m1 - m0) * NLO, SLOT, HALF)

    def combine_matrix(pick0, pick1):
        gate0, gate1 = gates[0:1, :].astype(F32), gates[1:2, :].astype(F32)
        return (jnp.where(pick0, gate0, 0.0) + jnp.where(pick1, gate1, 0.0)).T.astype(BF16)

    def mirrored(k):
        m, d = k // NLO, k % NLO
        return mirror(m) * NLO + (NLO - d) % NLO

    def wait_bytes(ref, sem):
        pltpu.make_async_copy(ref, ref, sem).wait()

    def moved(ref, number):
        first, end = MOVED[number]
        return ref.at[pl.ds(first, end - first)]

    def dispatch_copy(k, number):
        return pltpu.make_async_remote_copy(
            src_ref=outgoing.at[k],
            dst_ref=arrived.at[core, mirrored(k)],
            send_sem=disp_s.at[number],
            recv_sem=disp_r.at[mirror(k // NLO)],
            device_id=to(k // NLO, k % NLO),
            device_id_type=MESH,
        )

    def send_dispatch(number):
        def send(k, carry):
            first, end = MOVED[number]
            dispatch_copy(first + end - 1 - k, number).start()
            return carry

        lax.fori_loop(*MOVED[number], send, 0)

    near = picks(0, FIRST * NLO * SLOT)
    place(*near, 0, FIRST)
    pl.semaphore_wait(barrier, PEERS - 1 + 3 + 1)
    send_dispatch(NEAR)
    w_swap = pltpu.make_async_remote_copy(
        src_ref=fc_out.at[:, :, pl.ds(pl.multiple_of(other * HALF, HALF), HALF)],
        dst_ref=w_out.at[core],
        send_sem=swap_s,
        recv_sem=swap_r,
        device_id=sibling,
        device_id_type=MESH,
    )
    in_swap = pltpu.make_async_remote_copy(
        src_ref=fc_in,
        dst_ref=w_in.at[core],
        send_sem=hid_s,
        recv_sem=hid_r,
        device_id=sibling,
        device_id_type=MESH,
    )
    in_swap.start()
    w_swap.start()
    arrived[core, 0] = outgoing[0]
    far = picks(FIRST * NLO * SLOT, (NY - FIRST) * NLO * SLOT)
    place(*far, FIRST, NY)
    wait_bytes(moved(outgoing, NEAR), disp_s.at[NEAR])
    send_dispatch(FAR)
    combining[:, :FIRST * NLO * SLOT] = combine_matrix(*near)
    combining[:, FIRST * NLO * SLOT:] = combine_matrix(*far)

    def forward_copy(m):
        blocks = pl.ds(m * NLO, NLO)
        return pltpu.make_async_remote_copy(
            src_ref=arrived.at[core, blocks],
            dst_ref=arrived.at[core, blocks],
            send_sem=fwd_s.at[m],
            recv_sem=fwd_r.at[m],
            device_id=sibling,
            device_id_type=MESH,
        )

    def make_hidden(number):
        m0, m1 = SETS[number]

        def take(m, carry):
            wait_bytes(arrived.at[core, pl.ds(m * NLO, NLO)], disp_r.at[m])
            forward_copy(m).start()
            return carry

        if m0 == 0:
            wait_bytes(arrived.at[core, pl.ds(1, NLO - 1)], disp_r.at[0])
            forward_copy(0).start()
        lax.fori_loop(max(m0, 1), m1, take, 0)

        def relayout(m, carry):
            wait_bytes(arrived.at[other, pl.ds(m * NLO, NLO)], fwd_r.at[m])
            for h in range(2):
                block = arrived[h, pl.ds(m * NLO, NLO)].astype(F32)
                for i in range(2):
                    rows_in[i, pl.ds(pl.multiple_of(m * NLO * CAP, NLO * CAP), NLO * CAP), h * HALF:(h + 1) * HALF] = (
                        block[:, i * CAP:(i + 1) * CAP, :].reshape(NLO * CAP, HALF).astype(BF16)
                    )
            return carry

        lax.fori_loop(m0, m1, relayout, 0)
        rows = slice(m0 * NLO * CAP, m1 * NLO * CAP)
        if number == NEAR:
            loads[0].wait()
            in_swap.wait()
        for sec in range(2):
            for i in range(2):
                for n in range(0, HID, 256):
                    h = jnp.dot(rows_in[i, rows, :], w_in[sec, i, :, n:n + 256], preferred_element_type=F32)
                    hidden[sec, i, rows, n:n + 256] = jnp.maximum(h, 0.0).astype(BF16)
        if number == NEAR:
            loads[1].wait()
            w_swap.wait()

    def expert_outputs(m0, m1, ch):
        rows, cols = slice(m0 * NLO * CAP, m1 * NLO * CAP), slice(ch * CW, (ch + 1) * CW)
        sums = [
            jnp.dot(hidden[0, i, rows, :], w_out[0, i, :, cols], preferred_element_type=F32)
            + jnp.dot(hidden[1, i, rows, :], w_out[1, i, :, cols], preferred_element_type=F32)
            for i in range(2)
        ]
        sums = [s.reshape((m1 - m0) * NLO, CAP, CW) for s in sums]
        return jnp.concatenate(sums, axis=1).astype(BF16)

    def return_copy(ch, k, number):
        return pltpu.make_async_remote_copy(
            src_ref=part.at[ch, k],
            dst_ref=returned.at[ch, mirrored(k)],
            send_sem=ret_s.at[ch, number],
            recv_sem=ret_r.at[ch, number],
            device_id=to(k // NLO, k % NLO),
            device_id_type=MESH,
        )

    units = []

    def settle(left):
        while len(units) > left:
            ch, number = units.pop(0)
            wait_bytes(moved(part.at[ch], number), ret_s.at[ch, number])

    def send_back(ch, number):
        m0, m1 = SETS[number]
        part[ch, m0 * NLO:m1 * NLO] = expert_outputs(m0, m1, ch)
        settle(HOLD - 1)

        def send(k, carry):
            return_copy(ch, k, number).start()
            return carry

        lax.fori_loop(*MOVED[number], send, 0)
        units.append((ch, number))
        if number == NEAR:
            returned[ch, 0] = part[ch, 0]

    def scatter_copy(ch, r):
        return pltpu.make_async_remote_copy(
            src_ref=mixed_b.at[ch, (zhi + r) % 4],
            dst_ref=scattered.at[ch, r - 1],
            send_sem=rs_s.at[ch, r - 1],
            recv_sem=rs_r.at[ch, r - 1],
            device_id=to_hi(r),
            device_id_type=MESH,
        )

    def gather_copy(ch, r):
        return pltpu.make_async_remote_copy(
            src_ref=gathered.at[ch, core, zhi],
            dst_ref=gathered.at[ch, core, zhi],
            send_sem=ag_s.at[ch, r - 1],
            recv_sem=ag_r.at[ch, r - 1],
            device_id=to_hi(r),
            device_id_type=MESH,
        )

    def share_copy(ch):
        return pltpu.make_async_remote_copy(
            src_ref=gathered.at[ch, core],
            dst_ref=gathered.at[ch, core],
            send_sem=sib_s.at[ch],
            recv_sem=sib_r.at[ch],
            device_id=sibling,
            device_id_type=MESH,
        )

    quarter = ROWS // 4

    def scatter(ch):
        for number in (FAR, NEAR):
            wait_bytes(moved(returned.at[ch], number), ret_r.at[ch, number])
        mixed = jnp.dot(combining[...], returned[ch].reshape(slots, CW), preferred_element_type=F32)
        mixed = mixed.reshape(4, quarter, CW)
        mixed_f[ch] = mixed
        mixed_b[ch] = mixed.astype(BF16)
        for r in (2, 1, 3):
            scatter_copy(ch, r).start()

    def gather(ch):
        for r in range(1, 4):
            scatter_copy(ch, r).wait_recv()
        total = mixed_f[ch, zhi]
        for r in range(3):
            total = total + scattered[ch, r].astype(F32)
        gathered[ch, core, zhi] = total.astype(BF16)
        for r in (2, 1, 3):
            gather_copy(ch, r).start()

    def share(ch):
        for r in range(1, 4):
            gather_copy(ch, r).wait()
        share_copy(ch).start()

    make_hidden(NEAR)
    wait_bytes(moved(outgoing, FAR), disp_s.at[FAR])
    send_back(0, NEAR)
    make_hidden(FAR)
    send_back(0, FAR)
    send_back(1, NEAR)
    scatter(0)
    send_back(1, FAR)
    gather(0)
    scatter(1)
    share(0)
    gather(1)
    share(1)
    settle(0)
    for ch in range(NCH):
        share_copy(ch).wait()

    blocks = [(h, ch) for h in range(2) for ch in range(NCH)]
    spans = [slice(h * HALF + ch * CW, h * HALF + (ch + 1) * CW) for h, ch in blocks]
    summed = [
        tokens[:, span].astype(F32) + gathered[ch, h].reshape(ROWS, CW).astype(F32)
        for (h, ch), span in zip(blocks, spans)
    ]
    mean = sum(jnp.sum(s, axis=1, keepdims=True) for s in summed) / D
    centered = [s - mean for s in summed]
    spread = sum(jnp.sum(s * s, axis=1, keepdims=True) for s in centered) / D
    scale = lax.rsqrt(spread + 1e-05)
    for load in loads[2:]:
        load.wait()
    both = jnp.zeros((ROWS, 2 * HEAD_DIM), F32)
    for block, span in zip(centered, spans):
        memory = (block * scale * gain[:, span] + bias[:, span]).astype(BF16)
        both = both + jnp.dot(memory, kv[span, :], preferred_element_type=F32)
    keys, values = both[:, :HEAD_DIM].astype(BF16), both[:, HEAD_DIM:].astype(BF16)
    scores = lax.dot_general(queries[...], keys, (((1,), (1,)), ((), ())), preferred_element_type=F32)
    scores = scores * HEAD_DIM ** (-0.5)
    position = lax.broadcasted_iota(jnp.int32, (ROWS, ROWS), 1)
    scores = jnp.where(position < source_len[0], scores, -jnp.inf)
    expo = jnp.exp(scores - jnp.max(scores, axis=1, keepdims=True))
    weights = (expo / jnp.sum(expo, axis=1, keepdims=True)).astype(BF16)
    result = jnp.dot(weights, values, preferred_element_type=F32)
    row = lax.broadcasted_iota(jnp.int32, (ROWS, HEAD_DIM), 0)
    context[...] = jnp.where(row < target_len[0], result, 0.0).astype(BF16)

    def drain_forward(m, carry):
        wait_bytes(arrived.at[core, pl.ds(m * NLO, NLO)], fwd_s.at[m])
        return carry

    lax.fori_loop(0, NY, drain_forward, 0)
    for ch in range(NCH):
        for r in range(1, 4):
            scatter_copy(ch, r).wait_send()


def shards(
    tokens, routes, gates, fc_in, fc_out, norm_gain, norm_bias, key_weight, value_weight, queries,
    source_len, target_len,
):
    vmem = pl.BlockSpec(memory_space=pltpu.VMEM)
    smem = pl.BlockSpec(memory_space=pltpu.SMEM)
    hbm = pl.BlockSpec(memory_space=pl.ANY)
    dma = pltpu.SemaphoreType.DMA
    return pl.pallas_call(
        kernel,
        out_shape=jax.ShapeDtypeStruct((ROWS, HEAD_DIM), BF16),
        in_specs=[hbm, vmem, vmem, hbm, hbm, hbm, hbm, hbm, hbm, hbm, smem, smem],
        out_specs=vmem,
        scratch_shapes=[
            pltpu.VMEM((ROWS, D), BF16),
            pltpu.VMEM((1, D), F32),
            pltpu.VMEM((1, D), F32),
            pltpu.VMEM((ROWS, HEAD_DIM), BF16),
            pltpu.VMEM((PEERS, SLOT, HALF), BF16),
            pltpu.VMEM((2, PEERS, SLOT, HALF), BF16),
            pltpu.VMEM((2, PEERS * CAP, D), BF16),
            pltpu.VMEM((2, 2, D, HID), BF16),
            pltpu.VMEM((2, 2, HID, HALF), BF16),
            pltpu.VMEM((D, 2 * HEAD_DIM), BF16),
            pltpu.VMEM((2, 2, PEERS * CAP, HID), BF16),
            pltpu.VMEM((NCH, PEERS, SLOT, CW), BF16),
            pltpu.VMEM((NCH, PEERS, SLOT, CW), BF16),
            pltpu.VMEM((ROWS, PEERS * SLOT), BF16),
            pltpu.VMEM((NCH, 4, ROWS // 4, CW), F32),
            pltpu.VMEM((NCH, 4, ROWS // 4, CW), BF16),
            pltpu.VMEM((NCH, 3, ROWS // 4, CW), BF16),
            pltpu.VMEM((NCH, 2, 4, ROWS // 4, CW), BF16),
            dma((8,)),
            dma((2,)), dma((NY,)),
            dma((NY,)), dma((NY,)),
            dma, dma,
            dma, dma,
            dma((NCH, 2)), dma((NCH, 2)),
            dma((NCH, 3)), dma((NCH, 3)),
            dma((NCH, 3)), dma((NCH, 3)),
            dma((NCH,)), dma((NCH,)),
        ],
        compiler_params=pltpu.CompilerParams(
            collective_id=0, has_side_effects=True, vmem_limit_bytes=56 * 2**20
        ),
        cost_estimate=pl.CostEstimate(flops=2_300_000_000, bytes_accessed=10_000_000, transcendentals=20_000),
    )(
        tokens, routes.T, gates.T, fc_in, fc_out, norm_gain.reshape(1, -1), norm_bias.reshape(1, -1),
        key_weight, value_weight, queries, source_len, target_len,
    )


def solution(mesh):
    in_specs = (
        P(("dp", "expert"), None),
        P(("dp", "expert"), None),
        P(("dp", "expert"), None),
        P("expert", None, "section"),
        P("expert", "section", None),
        P(),
        P(),
        P(None, "section"),
        P(None, "section"),
        P(("dp", "expert"), "section"),
        P(("dp", "expert")),
        P(("dp", "expert")),
    )
    out_specs = P(("dp", "expert"), "section")
    return jax.shard_map(shards, mesh=mesh, in_specs=in_specs, out_specs=out_specs, check_vma=False)
```
